768 devices in a mesh: dp: 384 (over x, y, z), tensor: 2 (over core).
Axes of the slice: x: 4, y: 8, z: 12, core: 2. Of those that a mesh axis runs over, the one named last changes fastest.
Arguments:
- weight: float32 [6144, 9216], P('dp', 'tensor'), may hold values from -6 to 6
- momentum: float32 [6144, 9216], P('dp', 'tensor'), may hold values from -6 to 6
- grad: bfloat16 [6144, 9216], P('dp', 'tensor'), may hold values from -24 to 24
- right_factor: float32 [9216, 128], P('tensor'), may hold values from -0.0625 to 0.0625
Outputs:
- new_weight: float32 [6144, 9216], P('dp', 'tensor')
- new_momentum: float32 [6144, 9216], P('dp', 'tensor')
- new_factor: float32 [9216, 128], P('tensor')
The draws below stay inside these ranges and needn't reach their ends.
All inputs are finite; a program needn't handle non-finite values.
Results may differ from the reference program's by a relative error of at most 0.00075.
Values sent between devices are 32-bit elements; how exact they have to be, the bound alone decides.
No kernel may reach another device: no remote copies, remote signals or barrier semaphores. Data moves between devices by JAX's collectives and lax.ppermute only.
A program may use at most 32 MiB of HBM per device.

```python
import jax
import jax.numpy as jnp
from jax import lax

RANK = 128
M = 6144
N = 9216


def raised(array, key, source, target, shards_of, factor):
    def block_of(axis_at):
        return (jnp.arange(array.shape[axis_at]) // (array.shape[axis_at] // shards_of)).reshape((-1,) + (1,) * (array.ndim - 1 - axis_at))

    first = jax.random.permutation(key, shards_of)[block_of(target)]
    other_side = (block_of(target) + shards_of // 2) % shards_of
    return jnp.where((block_of(source) == first) | (block_of(source) == other_side), factor * array, array)


def block_levels(rng, dims, shards, smallest, largest):
    def one(axis_at, shards_of):
        heights = jax.random.uniform(jax.random.fold_in(jax.random.fold_in(rng, 6), axis_at), (shards_of,), jnp.float32, smallest / len(shards), largest / len(shards))
        return jnp.repeat(jnp.exp(heights), dims[axis_at] // shards_of).reshape((-1,) + (1,) * (len(dims) - axis_at - 1))

    gain = one(*shards[0])
    for cut in shards[1:]:
        gain = gain * one(*cut)
    return gain


def noise(key, dims, deviation, bound, split=(), held_as=jnp.bfloat16):
    entries = deviation * jax.random.normal(key, dims, jnp.float32)
    if split:
        entries = entries * block_levels(key, dims, split, -0.22, 0.18)
    return jnp.clip(entries, -bound, bound).astype(held_as)


def heavy_noise(own_key, extent, width, most, shards, heavy, kind=jnp.bfloat16):
    values = width * jax.random.normal(own_key, extent, jnp.float32)
    if shards:
        values = values * block_levels(own_key, extent, shards, -0.22, 0.18)
    return jnp.clip(raised(values, jax.random.fold_in(own_key, 3), *heavy), -most, most).astype(kind)


def setup_inputs(seed: int = 0) -> dict:
    keys = jax.random.split(jax.random.key(seed), 5)
    return {
        "weight": noise(keys[0], (M, N), 1.0, 6.0, ((0, 384), (1, 2)), jnp.float32),
        "momentum": noise(keys[1], (M, N), 1.0, 6.0, ((0, 384), (1, 2)), jnp.float32),
        "grad": heavy_noise(keys[2], (M, N), 1.0, 24.0, ((0, 384), (1, 2)), (0, 1, 384, 6.0)),
        "right_factor": noise(keys[3], (N, RANK), N ** -0.5, 0.0625, ((0, 2),), jnp.float32),
    }


PRECISE = lax.Precision.HIGHEST

def reference(weight, momentum, grad, right_factor):
    buffer = momentum + grad.astype(jnp.float32)
    left_raw = jnp.dot(buffer, right_factor, precision=PRECISE)
    gram = jnp.dot(left_raw.T, left_raw, precision=PRECISE)
    lower_factor = jnp.linalg.cholesky(gram)
    left = lax.linalg.triangular_solve(lower_factor, left_raw, left_side=False, lower=True, transpose_a=True)
    right = jnp.dot(buffer.T, left, precision=PRECISE)
    new_momentum = buffer - (1.0 - 0.95) * jnp.dot(left, right.T, precision=PRECISE)
    squares = lax.optimization_barrier(jnp.sum(right * right, axis=0))
    new_factor = right * lax.rsqrt(squares + 1e-06)
    factor_scale = 0.5 * (M * N / RANK) ** 0.5
    new_weight = weight - factor_scale * jnp.dot(left, new_factor.T, precision=PRECISE)
    return (new_weight, new_momentum, new_factor)
```

```python
import math

import jax
import jax.numpy as jnp
from jax import lax
from jax.sharding import Mesh
from jax.sharding import PartitionSpec as P

PRECISE = lax.Precision.HIGHEST
X, Y, Z = 4, 8, 12
RANK = 128


def gather(block, axis, size):
    return lax.all_to_all(
        jnp.broadcast_to(block[None], (size,) + block.shape), axis, 0, 0, tiled=True
    )


def per_device(weight, momentum, grad, right_factor):
    rows, cols = momentum.shape
    chunk = cols // Z
    piece = 2 * chunk // (X * Y)
    share = 2 * RANK // (2 * Y)
    y_at, z_at = lax.axis_index("y"), lax.axis_index("z")

    buffer = momentum + grad.astype(jnp.float32)
    left_raw = lax.psum(jnp.dot(buffer, right_factor, precision=PRECISE), "core")

    by_z = buffer.reshape(rows, Z, chunk).transpose(1, 0, 2)
    sent = jnp.concatenate([by_z, jnp.broadcast_to(left_raw[None], (Z, rows, RANK))], axis=2)
    held = lax.all_to_all(sent, "z", 0, 0, tiled=True).reshape(Z * rows, chunk + RANK)
    part = lax.dot_general(
        held, held[:, chunk:], (((0,), (0,)), ((), ())), precision=PRECISE
    )

    right_part = part[:chunk].reshape(X, Y // 2, 1, piece, RANK)
    right_part = jnp.broadcast_to(right_part, (X, Y // 2, 2, piece, RANK)).reshape(X * Y, piece, RANK)
    gram_part = lax.dynamic_slice_in_dim(part, chunk + (z_at % Y) * share, share, axis=0)
    gram_part = jnp.broadcast_to(gram_part[None], (X * Y, share, RANK))
    sent = jnp.concatenate([right_part, gram_part], axis=1)
    summed = jnp.sum(lax.all_to_all(sent, ("x", "y"), 0, 0, tiled=True), axis=0)

    by_z = gather(summed, "z", Z)
    gram = by_z[:Y, piece:].reshape(RANK, RANK)
    half = lax.dynamic_slice_in_dim(by_z, (y_at % 2) * (Z // 2), Z // 2, axis=0)[:, :piece]
    by_y = gather(half.reshape(-1, RANK), "y", Y).reshape(-1, RANK)
    by_x = gather(by_y, "x", X)
    right_raw = by_x.reshape(X * Y // 2, Z, piece, RANK).transpose(1, 0, 2, 3).reshape(cols, RANK)

    lower_factor = jnp.linalg.cholesky(gram)
    inverse = lax.linalg.triangular_solve(
        lower_factor, jnp.eye(RANK, dtype=jnp.float32), left_side=True, lower=True
    )
    left = jnp.dot(left_raw, inverse.T, precision=PRECISE)
    right = jnp.dot(right_raw, inverse.T, precision=PRECISE)
    squares = lax.psum(jnp.sum(right * right, axis=0), "core")
    scale = lax.rsqrt(squares + 1e-06)
    new_factor = right * scale
    new_momentum = buffer - (1.0 - 0.95) * jnp.dot(left, right.T, precision=PRECISE)
    factor_scale = 0.5 * math.sqrt(X * Y * Z * rows * 2 * cols / RANK)
    new_weight = weight - factor_scale * jnp.dot(left * scale, right.T, precision=PRECISE)
    return (new_weight, new_momentum, new_factor)


def solution(mesh):
    grid = Mesh(mesh.devices.reshape(X, Y, Z, 2), ("x", "y", "z", "core"))
    dp = ("x", "y", "z")
    in_specs = (P(dp, "core"), P(dp, "core"), P(dp, "core"), P("core", None))
    out_specs = (P(dp, "core"), P(dp, "core"), P("core", None))
    return jax.shard_map(
        per_device, mesh=grid, in_specs=in_specs, out_specs=out_specs, check_vma=False
    )
```

```python
import functools
import math

import jax
import jax.numpy as jnp
from jax import lax
from jax.experimental import pallas as pl
from jax.experimental.pallas import tpu as pltpu
from jax.sharding import Mesh
from jax.sharding import PartitionSpec as P

PRECISE = lax.Precision.HIGHEST
X, Y, Z = 4, 8, 12
RANK = 128
NT = (((1,), (1,)), ((), ()))
TN = (((0,), (0,)), ((), ()))
VM = pl.BlockSpec(memory_space=pltpu.VMEM)
SM = pl.BlockSpec(memory_space=pltpu.SMEM)


def params():
    return pltpu.CompilerParams(vmem_limit_bytes=32 * 1024 * 1024)


def factor_kernel(gram_ref, inverse_ref, work):
    step = 8
    row = lax.broadcasted_iota(jnp.int32, (RANK, RANK), 0)
    col = lax.broadcasted_iota(jnp.int32, (RANK, RANK), 1)
    work[:, :RANK] = gram_ref[...]
    work[:, RANK:] = (row == col).astype(jnp.float32)
    for at in range(0, RANK, step):
        block = work[at : at + step, :]
        rows = [block[i : i + 1, :] for i in range(step)]
        corner = block[:, at : at + step]
        entry = {
            (i, j): jnp.broadcast_to(corner[i : i + 1, j : j + 1], (1, RANK))
            for i in range(step) for j in range(i, step)
        }
        for i in range(step):
            scale = lax.rsqrt(entry[i, i])
            pivot = {j: entry[i, j] * scale for j in range(i + 1, step)}
            rows[i] = rows[i] * jnp.concatenate([scale, scale], axis=1)
            for j in range(i + 1, step):
                wide = jnp.concatenate([pivot[j], pivot[j]], axis=1)
                rows[j] = rows[j] - wide * rows[i]
                for k in range(j, step):
                    entry[j, k] = entry[j, k] - pivot[j] * pivot[k]
        done = jnp.concatenate(rows, axis=0)
        inverse_ref[at : at + step, :] = done[:, RANK:]
        if at + step < RANK:
            change = lax.dot_general(done[:, :RANK], done, TN, precision=PRECISE, preferred_element_type=jnp.float32)
            work[at + step :, :] = work[at + step :, :] - change[at + step :, :]

def factor(gram):
    return pl.pallas_call(factor_kernel, out_shape=jax.ShapeDtypeStruct((RANK,RANK),jnp.float32),
        in_specs=[VM], out_specs=VM, scratch_shapes=[pltpu.VMEM((RANK,2*RANK),jnp.float32)],
        compiler_params=params(), name="factor")(gram)

def order_kernel(pieces, shares, by_y_ref, right_ref, gram_ref):
    Y, Z, piece, share = by_y_ref.shape[0], pieces[0], pieces[1], shares
    pitch = piece + share
    for y in range(Y):
        for z in range(Z):
            right_ref[(z*Y+y)*piece:(z*Y+y+1)*piece, :] = by_y_ref[y, z*pitch:z*pitch+piece, :]
        for z in range(4):
            gram_ref[(y*4+z)*share:(y*4+z+1)*share, :] = by_y_ref[y, z*pitch+piece:(z+1)*pitch, :]

def order(by_y):
    return pl.pallas_call(functools.partial(order_kernel,(12,12),4),
        out_shape=(jax.ShapeDtypeStruct((1152,RANK),jnp.float32),jax.ShapeDtypeStruct((RANK,RANK),jnp.float32)),
        in_specs=[VM],out_specs=(VM,VM),compiler_params=params(),name="order")(by_y)

def split(value):
    high = value.astype(jnp.bfloat16)
    return high, (value - high.astype(jnp.float32)).astype(jnp.bfloat16)

def right_kernel(at_ref, b0, b1, b2, b3, inverse_ref, left_raw_ref, right_ref, squares_ref, left_ref):
    X, Z, piece = 4, 12, 96
    inverse = inverse_ref[...]
    left_ref[...] = lax.dot_general(left_raw_ref[...], inverse, NT, precision=PRECISE, preferred_element_type=jnp.float32)
    high, low = split(inverse)
    factors = jnp.concatenate([jnp.concatenate([high, high], axis=1),
        jnp.concatenate([low, jnp.zeros_like(low)], axis=1)], axis=0)
    total = jnp.zeros((8, RANK), jnp.float32)
    for back, block in enumerate((b0, b1, b2, b3)):
        x = lax.rem(at_ref[0] + (X - back), X)
        for z in range(Z):
            both = jnp.concatenate(split(block[z*piece:(z+1)*piece, :]), axis=1)
            out = lax.dot_general(both, factors, NT, preferred_element_type=jnp.float32)
            out = out[:, :RANK] + out[:, RANK:]
            right_ref[pl.ds(pl.multiple_of(z*X*piece + x*piece, 8), piece), :] = out
            total = total + jnp.sum((out*out).reshape(piece//8, 8, RANK), axis=0)
    squares_ref[...] = jnp.sum(total, axis=0, keepdims=True)

def right_of(at, blocks, inverse, left_raw):
    return pl.pallas_call(right_kernel,
        out_shape=(jax.ShapeDtypeStruct((4608,RANK),jnp.float32),jax.ShapeDtypeStruct((1,RANK),jnp.float32),jax.ShapeDtypeStruct((16,RANK),jnp.float32)),
        in_specs=[SM]+[VM]*6,out_specs=(VM,VM,VM),compiler_params=params(),name="right")(at,*blocks,inverse,left_raw)

def update_kernel(decay, gain, right_ref, squares_ref, left_ref, buffer_ref, weight_ref, weight_out, momentum_out, factor_out):
    tile = 512
    scale = lax.rsqrt(squares_ref[...] + 1e-06)
    left = left_ref[...]
    high, low = split(jnp.concatenate([decay*left, (gain*left)*scale], axis=0))
    both_left = jnp.concatenate([jnp.concatenate([high, high], axis=1), jnp.concatenate([low, jnp.zeros_like(low)], axis=1)], axis=0)
    n = left.shape[0]
    for at in range(0, right_ref.shape[0], tile):
        right = right_ref[at:at+tile, :]
        factor_out[at:at+tile, :] = right * scale
        both = jnp.concatenate(split(right), axis=1)
        out = lax.dot_general(both_left, both, NT, preferred_element_type=jnp.float32)
        out = out[:2*n] + out[2*n:]
        momentum_out[:, at:at+tile] = buffer_ref[:, at:at+tile] - out[:n]
        weight_out[:, at:at+tile] = weight_ref[:, at:at+tile] - out[n:]

def update(decay, gain, right, squares, left, buffer, weight):
    return pl.pallas_call(functools.partial(update_kernel,decay,gain),
        out_shape=(jax.ShapeDtypeStruct(weight.shape,jnp.float32),jax.ShapeDtypeStruct(weight.shape,jnp.float32),jax.ShapeDtypeStruct(right.shape,jnp.float32)),
        in_specs=[VM]*5,out_specs=(VM,VM,VM),compiler_params=params(),name="update")(right,squares,left,buffer,weight)


def gather(block, axis, size):
    return lax.all_to_all(
        jnp.broadcast_to(block[None], (size,) + block.shape), axis, 0, 0, tiled=True
    )


def per_device(weight, momentum, grad, right_factor):
    rows, cols = momentum.shape
    chunk = cols // Z
    piece = chunk // (X * Y)
    share = RANK // (4 * Y)
    x_at, z_at = lax.axis_index("x"), lax.axis_index("z")

    buffer = momentum + grad.astype(jnp.float32)
    left_raw = lax.psum(jnp.dot(buffer, right_factor, precision=PRECISE), "core")

    by_z = buffer.reshape(rows, Z, chunk).transpose(1, 0, 2)
    sent = jnp.concatenate([by_z, jnp.broadcast_to(left_raw[None], (Z, rows, RANK))], axis=2)
    held = lax.all_to_all(sent, "z", 0, 0, tiled=True).reshape(Z * rows, chunk + RANK)
    part = lax.dot_general(held, held[:, chunk:], TN, precision=PRECISE)

    right_part = part[:chunk].reshape(X * Y, piece, RANK)
    gram_part = part[chunk:].reshape(Y, 4, share, RANK)
    gram_part = lax.dynamic_index_in_dim(gram_part, z_at % 4, axis=1, keepdims=False)
    gram_part = jnp.broadcast_to(gram_part[None], (X, Y, share, RANK)).reshape(X * Y, share, RANK)
    sent = jnp.concatenate([right_part, gram_part], axis=1)
    summed = jnp.sum(lax.all_to_all(sent, ("x", "y"), 0, 0, tiled=True), axis=0)

    by_z = gather(summed, "z", Z).reshape(-1, RANK)
    by_y = gather(by_z, "y", Y)
    own, gram = order(by_y)
    blocks = [own] + [
        lax.ppermute(own, "x", [(i, (i + k) % X) for i in range(X)]) for k in range(1, X)
    ]
    inverse = factor(gram)
    right, squares, left = right_of(x_at.reshape(1), blocks, inverse, left_raw)
    squares = lax.psum(squares, "core")
    gain = 0.5 * math.sqrt(X * Y * Z * rows * 2 * cols / RANK)
    return update(1.0 - 0.95, gain, right, squares, left, buffer, weight)


def solution(mesh):
    grid = Mesh(mesh.devices.reshape(X, Y, Z, 2), ("x", "y", "z", "core"))
    dp = ("x", "y", "z")
    in_specs = (P(dp, "core"), P(dp, "core"), P(dp, "core"), P("core", None))
    out_specs = (P(dp, "core"), P(dp, "core"), P("core", None))
    return jax.shard_map(
        per_device, mesh=grid, in_specs=in_specs, out_specs=out_specs, check_vma=False
    )
```

```python
import functools
import math

import jax
import jax.numpy as jnp
from jax import lax
from jax.experimental import pallas as pl
from jax.experimental.pallas import tpu as pltpu
from jax.sharding import Mesh
from jax.sharding import PartitionSpec as P

PRECISE = lax.Precision.HIGHEST
X, J, K, B = 4, 4, 6, 2
NEAR, FAR = ("x", "yb", "zb"), ("yj", "zk")
RANK = 128
NT = (((1,), (1,)), ((), ()))
TN = (((0,), (0,)), ((), ()))
VM = pl.BlockSpec(memory_space=pltpu.VMEM)


def params():
    return pltpu.CompilerParams(vmem_limit_bytes=16 * 1024 * 1024)


def factor_kernel(gram_ref, inverse_ref, work):
    step = 8
    row = lax.broadcasted_iota(jnp.int32, (RANK, RANK), 0)
    col = lax.broadcasted_iota(jnp.int32, (RANK, RANK), 1)
    half = RANK // 2
    rest = gram_ref[half:, :]
    nothing = jnp.zeros((half // 2, half), jnp.float32)
    work[:half, :RANK] = gram_ref[:half, :]
    work[half : half + half // 2, :RANK] = jnp.concatenate([nothing, rest[:, :half]], axis=1)
    work[half + half // 2 :, :RANK] = jnp.concatenate([nothing, rest[:, half:]], axis=1)
    work[:, RANK:] = (row == col).astype(jnp.float32)
    for at in range(0, RANK, step):
        block = work[at : at + step, :]
        rows = [block[i : i + 1, :] for i in range(step)]
        corner = block[:, at : at + step]
        entry = {
            (i, j): jnp.broadcast_to(corner[i : i + 1, j : j + 1], (1, RANK))
            for i in range(step) for j in range(i, step)
        }
        for i in range(step):
            scale = lax.rsqrt(entry[i, i])
            pivot = {j: entry[i, j] * scale for j in range(i + 1, step)}
            rows[i] = rows[i] * jnp.concatenate([scale, scale], axis=1)
            for j in range(i + 1, step):
                wide = jnp.concatenate([pivot[j], pivot[j]], axis=1)
                rows[j] = rows[j] - wide * rows[i]
                for k in range(j, step):
                    entry[j, k] = entry[j, k] - pivot[j] * pivot[k]
        done = jnp.concatenate(rows, axis=0)
        inverse_ref[at : at + step, :] = done[:, RANK:]
        if at + step < RANK:
            change = lax.dot_general(done[:, :RANK], done, TN, precision=PRECISE, preferred_element_type=jnp.float32)
            work[at + step :, :] = work[at + step :, :] - change[at + step :, :]

def factor(gram):
    return pl.pallas_call(factor_kernel, out_shape=jax.ShapeDtypeStruct((RANK,RANK),jnp.float32),
        in_specs=[VM], out_specs=VM, scratch_shapes=[pltpu.VMEM((RANK,2*RANK),jnp.float32)],
        compiler_params=params(), name="factor")(gram)

def split(value):
    high = value.astype(jnp.bfloat16)
    return high, (value - high.astype(jnp.float32)).astype(jnp.bfloat16)

def right_kernel(raw_ref, inverse_ref, left_raw_ref, right_ref, squares_ref, left_ref):
    tile = 512
    inverse = inverse_ref[...]
    left_ref[...] = lax.dot_general(
        left_raw_ref[...], inverse, NT, precision=PRECISE, preferred_element_type=jnp.float32
    )
    high, low = split(inverse)
    factors = jnp.concatenate(
        [
            jnp.concatenate([high, high], axis=1),
            jnp.concatenate([low, jnp.zeros_like(low)], axis=1),
        ],
        axis=0,
    )
    total = jnp.zeros((8, RANK), jnp.float32)
    for at in range(0, raw_ref.shape[0], tile):
        both = jnp.concatenate(split(raw_ref[at : at + tile, :]), axis=1)
        out = lax.dot_general(both, factors, NT, preferred_element_type=jnp.float32)
        out = out[:, :RANK] + out[:, RANK:]
        right_ref[at : at + tile, :] = out
        total = total + jnp.sum((out * out).reshape(tile // 8, 8, RANK), axis=0)
    squares_ref[...] = jnp.sum(total, axis=0, keepdims=True)


def right_of(raw, inverse, left_raw):
    return pl.pallas_call(
        right_kernel,
        out_shape=(
            jax.ShapeDtypeStruct(raw.shape, jnp.float32),
            jax.ShapeDtypeStruct((1, RANK), jnp.float32),
            jax.ShapeDtypeStruct(left_raw.shape, jnp.float32),
        ),
        in_specs=[VM] * 3,
        out_specs=(VM, VM, VM),
        compiler_params=params(),
        name="right",
    )(raw, inverse, left_raw)


def update_kernel(
    decay, gain, right_ref, squares_ref, other_ref, left_ref, buffer_ref, weight_ref,
    weight_out, momentum_out, factor_out,
):
    tile = 512
    scale = lax.rsqrt((squares_ref[...] + other_ref[...]) + 1e-06)
    left = left_ref[...]
    high, low = split(jnp.concatenate([decay * left, (gain * left) * scale], axis=0))
    both_left = jnp.concatenate(
        [
            jnp.concatenate([high, high], axis=1),
            jnp.concatenate([low, jnp.zeros_like(low)], axis=1),
        ],
        axis=0,
    )
    n = left.shape[0]
    for at in range(0, right_ref.shape[0], tile):
        right = right_ref[at : at + tile, :]
        factor_out[at : at + tile, :] = right * scale
        both = jnp.concatenate(split(right), axis=1)
        out = lax.dot_general(both_left, both, NT, preferred_element_type=jnp.float32)
        out = out[: 2 * n] + out[2 * n :]
        momentum_out[:, at : at + tile] = buffer_ref[:, at : at + tile] - out[:n]
        weight_out[:, at : at + tile] = weight_ref[:, at : at + tile] - out[n:]


def update(decay, gain, right, squares, other, left, buffer, weight):
    return pl.pallas_call(
        functools.partial(update_kernel, decay, gain),
        out_shape=(
            jax.ShapeDtypeStruct(weight.shape, jnp.float32),
            jax.ShapeDtypeStruct(weight.shape, jnp.float32),
            jax.ShapeDtypeStruct(right.shape, jnp.float32),
        ),
        in_specs=[VM] * 6,
        out_specs=(VM, VM, VM),
        compiler_params=params(),
        name="update",
    )(right, squares, other, left, buffer, weight)


def gather(block, axis, size):
    return lax.all_to_all(
        jnp.broadcast_to(block[None], (size,) + block.shape), axis, 0, 0, tiled=True
    )


def packed(gram):
    half = RANK // 2
    corner = gram[half:, half:]
    corner = jnp.concatenate([corner[: half // 2], corner[half // 2 :]], axis=1)
    return jnp.concatenate([gram[:half], corner], axis=0)


def per_device(weight, momentum, grad, right_factor):
    rows, cols = momentum.shape
    near, far = X * B * B, J * K
    chunk = cols // near
    wide = -(-chunk // RANK) * RANK
    piece = chunk // far

    buffer = momentum + grad.astype(jnp.float32)
    left_raw = lax.psum(jnp.dot(buffer, right_factor, precision=PRECISE), "core")

    parts = buffer.reshape(rows, near, chunk).transpose(1, 0, 2)
    parts = jnp.pad(parts, ((0, 0), (0, 0), (0, wide - chunk)))
    sent = jnp.concatenate(
        [parts, jnp.broadcast_to(left_raw[None], (near, rows, RANK))], axis=2
    )
    held = lax.all_to_all(sent, NEAR, 0, 0, tiled=True).reshape(near * rows, wide + RANK)
    part = lax.dot_general(held, held[:, wide:], TN, precision=PRECISE)

    sent = jnp.concatenate(
        [
            part[:chunk].reshape(far, piece, RANK),
            packed(part[wide:]).reshape(far, -1, RANK),
        ],
        axis=1,
    )
    summed = jnp.sum(lax.all_to_all(sent, FAR, 0, 0, tiled=True), axis=0)

    by_far = gather(summed, FAR, far)
    gram = by_far[:, piece:].reshape(-1, RANK)
    right_raw = gather(by_far[:, :piece].reshape(chunk, RANK), NEAR, near).reshape(cols, RANK)
    right, squares, left = right_of(right_raw, factor(gram), left_raw)
    other = lax.ppermute(squares, "core", [(0, 1), (1, 0)])
    gain = 0.5 * math.sqrt(near * far * rows * 2 * cols / RANK)
    return update(1.0 - 0.95, gain, right, squares, other, left, buffer, weight)


def solution(mesh):
    dp = ("x", "yj", "yb", "zk", "zb")
    grid = Mesh(mesh.devices.reshape(X, J, B, K, B, 2), dp + ("core",))
    in_specs = (P(dp, "core"), P(dp, "core"), P(dp, "core"), P("core", None))
    out_specs = (P(dp, "core"), P(dp, "core"), P("core", None))
    return jax.shard_map(
        per_device, mesh=grid, in_specs=in_specs, out_specs=out_specs, check_vma=False
    )
```

```python
import functools
import math

import jax
import jax.numpy as jnp
from jax import lax
from jax.experimental import pallas as pl
from jax.experimental.pallas import tpu as pltpu
from jax.sharding import PartitionSpec as P

PRECISE = lax.Precision.HIGHEST
X, Y, Z = 4, 8, 12
ALL = ("dp", "tensor")
RANK = 128
NT = (((1,), (1,)), ((), ()))
TN = (((0,), (0,)), ((), ()))
VM = pl.BlockSpec(memory_space=pltpu.VMEM)
SM = pl.BlockSpec(memory_space=pltpu.SMEM)


def params():
    return pltpu.CompilerParams(vmem_limit_bytes=16 * 1024 * 1024)


def split(value, parts=2):
    out = []
    for _ in range(parts):
        out.append(value.astype(jnp.bfloat16))
        value = value - out[-1].astype(jnp.float32)
    return out


def inverse_factor(gram, store):
    step = 16
    row = lax.broadcasted_iota(jnp.int32, (RANK, RANK), 0)
    col = lax.broadcasted_iota(jnp.int32, (RANK, RANK), 1)
    rest = jnp.concatenate([gram, (row == col).astype(jnp.float32)], axis=1)
    for at in range(0, RANK, step):
        rows = [rest[i : i + 1, :] for i in range(step)]
        corner = rest[:step, at : at + step]
        entry = {
            (i, j): jnp.broadcast_to(corner[i : i + 1, j : j + 1], (1, RANK))
            for i in range(step)
            for j in range(i, step)
        }
        for i in range(step):
            scale = lax.rsqrt(entry[i, i])
            pivot = {j: entry[i, j] * scale for j in range(i + 1, step)}
            rows[i] = rows[i] * jnp.concatenate([scale, scale], axis=1)
            for j in range(i + 1, step):
                rows[j] = rows[j] - jnp.concatenate([pivot[j], pivot[j]], axis=1) * rows[i]
                for k in range(j, step):
                    entry[j, k] = entry[j, k] - pivot[j] * pivot[k]
        done = jnp.concatenate(rows, axis=0)
        store(at, done[:, RANK:])
        if at + step < RANK:
            l1, l2, l3 = split(done[:, :RANK], 3)
            r1, r2, r3 = split(done, 3)
            change = lax.dot_general(
                jnp.concatenate([l1, l1, l2, l2, l1, l3], axis=0),
                jnp.concatenate([r1, r2, r1, r2, r3, r1], axis=0),
                TN,
                preferred_element_type=jnp.float32,
            )
            rest = rest[step:] - change[at + step :]


def factor_kernel(packed_ref, inverse_ref):
    half = RANK // 2
    rest = packed_ref[half:, :]
    nothing = jnp.zeros((half // 2, half), jnp.float32)
    gram = jnp.concatenate(
        [
            packed_ref[:half, :],
            jnp.concatenate([nothing, rest[:, :half]], axis=1),
            jnp.concatenate([nothing, rest[:, half:]], axis=1),
        ],
        axis=0,
    )

    def store(at, rows):
        inverse_ref[at : at + rows.shape[0], :] = rows

    inverse_factor(gram, store)


def factor(packed_gram):
    return pl.pallas_call(
        factor_kernel,
        out_shape=jax.ShapeDtypeStruct((RANK, RANK), jnp.float32),
        in_specs=[VM],
        out_specs=VM,
        compiler_params=params(),
        name="factor",
    )(packed_gram)


def right_kernel(at_ref, own_ref, other_ref, inverse_ref, left_raw_ref, right_ref, squares_ref, left_ref):
    rows = own_ref.shape[0]
    inverse = inverse_ref[...]
    left_ref[...] = lax.dot_general(
        left_raw_ref[...], inverse, NT, precision=PRECISE, preferred_element_type=jnp.float32
    )
    squares = jnp.zeros((8, RANK), jnp.float32)
    for place, raw in ((at_ref[0], own_ref), (1 - at_ref[0], other_ref)):
        right = lax.dot_general(
            raw[...], inverse, NT, precision=PRECISE, preferred_element_type=jnp.float32
        )
        right_ref[pl.ds(pl.multiple_of(place * rows, 8), rows), :] = right
        squares = squares + jnp.sum((right * right).reshape(-1, 8, RANK), axis=0)
    squares_ref[...] = squares


def right_of(at, own, other, inverse, left_raw):
    return pl.pallas_call(
        right_kernel,
        out_shape=(
            jax.ShapeDtypeStruct((2 * own.shape[0], RANK), jnp.float32),
            jax.ShapeDtypeStruct((8, RANK), jnp.float32),
            jax.ShapeDtypeStruct(left_raw.shape, jnp.float32),
        ),
        in_specs=[SM] + [VM] * 4,
        out_specs=(VM, VM, VM),
        compiler_params=params(),
        name="right",
    )(at, own, other, inverse, left_raw)


def update_kernel(
    decay, gain, right_ref, left_ref, buffer_ref, weight_ref, weight_out, momentum_out, factor_out
):
    near, pitch, _ = right_ref.shape
    chunk, group = pitch - 8, 2
    squares = right_ref[0, chunk:, :]
    for k in range(1, near):
        squares = squares + right_ref[k, chunk:, :]
    scale = lax.rsqrt(jnp.sum(squares, axis=0, keepdims=True) + 1e-06)
    left = left_ref[...]
    high, low = split(jnp.concatenate([decay * left, (gain * left) * scale], axis=0))
    both_left = jnp.concatenate(
        [
            jnp.concatenate([high, high], axis=1),
            jnp.concatenate([low, jnp.zeros_like(low)], axis=1),
        ],
        axis=0,
    )
    n = left.shape[0]
    for first in range(0, near, group):
        right = jnp.concatenate([right_ref[first + k, :chunk, :] for k in range(group)], axis=0)
        at, end = first * chunk, (first + group) * chunk
        factor_out[at:end, :] = right * scale
        both = jnp.concatenate(split(right), axis=1)
        out = lax.dot_general(both_left, both, NT, preferred_element_type=jnp.float32)
        out = out[: 2 * n] + out[2 * n :]
        momentum_out[:, at:end] = buffer_ref[:, at:end] - out[:n]
        weight_out[:, at:end] = weight_ref[:, at:end] - out[n:]


def update(decay, gain, right, left, buffer, weight):
    return pl.pallas_call(
        functools.partial(update_kernel, decay, gain),
        out_shape=(
            jax.ShapeDtypeStruct(weight.shape, jnp.float32),
            jax.ShapeDtypeStruct(weight.shape, jnp.float32),
            jax.ShapeDtypeStruct((weight.shape[1], RANK), jnp.float32),
        ),
        in_specs=[VM] * 4,
        out_specs=(VM, VM, VM),
        compiler_params=params(),
        name="update",
    )(right, left, buffer, weight)


def groups(same, order):
    found = {}
    for device in range(X * Y * Z * 2):
        chip, core = divmod(device, 2)
        x, y, z = shifted(chip, core)
        found.setdefault((core, same(x, y, z)), []).append((order(x, y, z), device))
    return [[device for _, device in sorted(members)] for members in found.values()]


def shifted(chip, core):
    return (chip // (Y * Z) + core) % X, (chip // Z % Y + core) % Y, (chip % Z + core) % Z


def cube(x, y, z):
    return x % 2, y % 2, z % 2


def far(x, y, z):
    return y // 2, z // 2


CUBE = groups(lambda x, y, z: (x // 2, y // 2, z // 2), cube)
NEAR = groups(far, lambda x, y, z: cube(x, y, z) + (x // 2,))
FAR = groups(lambda x, y, z: cube(x, y, z) + (x // 2,), far)


def exchange(blocks, members):
    return lax.all_to_all(blocks, ALL, 0, 0, axis_index_groups=members, tiled=True)


def gather(block, members):
    return exchange(jnp.broadcast_to(block[None], (len(members[0]),) + block.shape), members)


def packed(gram):
    half = RANK // 2
    corner = gram[half:, half:]
    corner = jnp.concatenate([corner[: half // 2], corner[half // 2 :]], axis=1)
    return jnp.concatenate([gram[:half], corner], axis=0)


def per_device(weight, momentum, grad, right_factor):
    rows, cols = momentum.shape
    n_near, n_far = len(NEAR[0]), len(FAR[0])
    chunk = cols // n_near
    wide = -(-chunk // RANK) * RANK
    piece = chunk // n_far

    buffer = momentum + grad.astype(jnp.float32)
    left_raw = lax.psum(jnp.dot(buffer, right_factor, precision=PRECISE), "tensor")

    parts = buffer.reshape(rows, n_near, chunk).transpose(1, 0, 2)
    parts = jnp.pad(parts, ((0, 0), (0, 0), (0, wide - chunk)))
    beside = jnp.broadcast_to(left_raw[None], (n_near, rows, RANK))
    held = exchange(jnp.concatenate([parts, beside], axis=2), NEAR)
    held = held.reshape(n_near * rows, wide + RANK)
    part = lax.dot_general(held, held[:, wide:], TN, precision=PRECISE)

    sent = jnp.concatenate(
        [
            part[:chunk].reshape(n_far, piece, RANK),
            packed(part[wide:]).reshape(n_far, -1, RANK),
        ],
        axis=1,
    )
    summed = jnp.sum(exchange(sent, FAR), axis=0)

    by_far = gather(summed, FAR)
    own = by_far[:, :piece].reshape(chunk, RANK)
    count = X * Y * Z
    other = lax.ppermute(own, "dp", [(i, (i + count // 2) % count) for i in range(count)])
    inverse = factor(by_far[:, piece:].reshape(-1, RANK))
    x = (lax.axis_index("dp") // (Y * Z) + lax.axis_index("tensor")) % X
    right, squares, left = right_of((x // 2).reshape(1), own, other, inverse, left_raw)
    squares = lax.psum(squares, "tensor")
    by_cube = gather(jnp.concatenate([right, squares], axis=0), CUBE)
    gain = 0.5 * math.sqrt(count * rows * 2 * cols / RANK)
    return update(1.0 - 0.95, gain, by_cube, left, buffer, weight)


def solution(mesh):
    in_specs = (P("dp", "tensor"), P("dp", "tensor"), P("dp", "tensor"), P("tensor", None))
    out_specs = (P("dp", "tensor"), P("dp", "tensor"), P("tensor", None))
    return jax.shard_map(
        per_device, mesh=mesh, in_specs=in_specs, out_specs=out_specs, check_vma=False
    )
```

```python
import functools
import math

import jax
import jax.numpy as jnp
from jax import lax
from jax.experimental import pallas as pl
from jax.experimental.pallas import tpu as pltpu
from jax.sharding import PartitionSpec as P

PRECISE = lax.Precision.HIGHEST
X, Y, Z = 4, 8, 12
ALL = ("dp", "tensor")
RANK = 128
NT = (((1,), (1,)), ((), ()))
TN = (((0,), (0,)), ((), ()))
VM = pl.BlockSpec(memory_space=pltpu.VMEM)
SM = pl.BlockSpec(memory_space=pltpu.SMEM)
ANY = pl.BlockSpec(memory_space=pl.ANY)


def params():
    return pltpu.CompilerParams(vmem_limit_bytes=16 * 1024 * 1024)


def split(value, parts=2):
    out = []
    for _ in range(parts):
        out.append(value.astype(jnp.bfloat16))
        value = value - out[-1].astype(jnp.float32)
    return out


def head_kernel(buffer_ref, factor_ref, parts_ref, left_ref):
    n_parts, rows, wide = parts_ref.shape
    chunk = buffer_ref.shape[1] // n_parts
    zeros = jnp.zeros((rows, wide - chunk), jnp.float32)
    for k in range(n_parts):
        part = buffer_ref[:, k * chunk : (k + 1) * chunk]
        parts_ref[k, :, :] = jnp.concatenate([part, zeros], axis=1)
    b1, b2 = split(buffer_ref[...])
    f1, f2 = split(factor_ref[...])
    both = jnp.dot(jnp.concatenate([b1, b2], axis=0), f1, preferred_element_type=jnp.float32)
    small = both[rows:] + jnp.dot(b1, f2, preferred_element_type=jnp.float32)
    left_ref[...] = small + both[:rows]


def head(buffer, right_factor, n_parts, wide):
    rows = buffer.shape[0]
    return pl.pallas_call(
        head_kernel,
        out_shape=(
            jax.ShapeDtypeStruct((n_parts, rows, wide), jnp.float32),
            jax.ShapeDtypeStruct((rows, RANK), jnp.float32),
        ),
        in_specs=[VM, VM],
        out_specs=(VM, VM),
        compiler_params=params(),
        name="head",
    )(buffer, right_factor)


def part_kernel(piece, held_ref, sent_ref, part):
    n, pitch, _ = sent_ref.shape
    wide, share, half = held_ref.shape[1] - RANK, pitch - piece, RANK // 2
    h1, h2 = split(held_ref[...])
    l1, l2 = h1[:, wide:], h2[:, wide:]
    product = lax.dot_general(
        jnp.concatenate([h2, h1, h1], axis=0),
        jnp.concatenate([l1, l2, l1], axis=0),
        TN,
        preferred_element_type=jnp.float32,
    )
    part[...] = product[: n * piece]
    corner = product[wide + half :, half:]
    corner = jnp.concatenate([corner[: half // 2], corner[half // 2 :]], axis=1)
    packed = jnp.concatenate([product[wide : wide + half], corner], axis=0)
    for k in range(n):
        sent_ref[k, :piece, :] = part[k * piece : (k + 1) * piece, :]
        sent_ref[k, piece:, :] = packed[k * share : (k + 1) * share, :]


def part_of(held, n, piece):
    share = (RANK // 2 + RANK // 4) // n
    return pl.pallas_call(
        functools.partial(part_kernel, piece),
        out_shape=jax.ShapeDtypeStruct((n, piece + share, RANK), jnp.float32),
        in_specs=[VM],
        out_specs=VM,
        scratch_shapes=[pltpu.VMEM((n * piece, RANK), jnp.float32)],
        compiler_params=params(),
        name="part",
    )(held)


def inverse_factor(gram, store):
    step = 16
    row = lax.broadcasted_iota(jnp.int32, (RANK, RANK), 0)
    col = lax.broadcasted_iota(jnp.int32, (RANK, RANK), 1)
    rest = jnp.concatenate([gram, (row == col).astype(jnp.float32)], axis=1)
    for at in range(0, RANK, step):
        rows = [rest[i : i + 1, :] for i in range(step)]
        corner = rest[:step, at : at + step]
        entry = {
            (i, j): jnp.broadcast_to(corner[i : i + 1, j : j + 1], (1, RANK))
            for i in range(step)
            for j in range(i, step)
        }
        for i in range(step):
            scale = lax.rsqrt(entry[i, i])
            pivot = {j: entry[i, j] * scale for j in range(i + 1, step)}
            rows[i] = rows[i] * jnp.concatenate([scale, scale], axis=1)
            for j in range(i + 1, step):
                rows[j] = rows[j] - jnp.concatenate([pivot[j], pivot[j]], axis=1) * rows[i]
                for k in range(j, step):
                    entry[j, k] = entry[j, k] - pivot[j] * pivot[k]
        done = jnp.concatenate(rows, axis=0)
        store(at, done[:, RANK:])
        if at + step < RANK:
            l1, l2, l3 = split(done[:, :RANK], 3)
            r1, r2, r3 = split(done, 3)
            change = lax.dot_general(
                jnp.concatenate([l1, l1, l2, l2, l1, l3], axis=0),
                jnp.concatenate([r1, r2, r1, r2, r3, r1], axis=0),
                TN,
                preferred_element_type=jnp.float32,
            )
            rest = rest[step:] - change[at + step :]


def factor_kernel(packed_ref, inverse_ref):
    half = RANK // 2
    rest = packed_ref[half:, :]
    nothing = jnp.zeros((half // 2, half), jnp.float32)
    gram = jnp.concatenate(
        [
            packed_ref[:half, :],
            jnp.concatenate([nothing, rest[:, :half]], axis=1),
            jnp.concatenate([nothing, rest[:, half:]], axis=1),
        ],
        axis=0,
    )

    def store(at, rows):
        inverse_ref[at : at + rows.shape[0], :] = rows

    inverse_factor(gram, store)


def factor(packed_gram):
    return pl.pallas_call(
        factor_kernel,
        out_shape=jax.ShapeDtypeStruct((RANK, RANK), jnp.float32),
        in_specs=[VM],
        out_specs=VM,
        compiler_params=params(),
        name="factor",
    )(packed_gram)


def right_kernel(at_ref, own_ref, other_ref, inverse_ref, left_raw_ref, right_ref, squares_ref, left_ref):
    rows = own_ref.shape[0]
    inverse = inverse_ref[...]
    left_ref[...] = lax.dot_general(
        left_raw_ref[...], inverse, NT, precision=PRECISE, preferred_element_type=jnp.float32
    )
    squares = jnp.zeros((8, RANK), jnp.float32)
    for place, raw in ((at_ref[0], own_ref), (1 - at_ref[0], other_ref)):
        right = lax.dot_general(
            raw[...], inverse, NT, precision=PRECISE, preferred_element_type=jnp.float32
        )
        right_ref[pl.ds(pl.multiple_of(place * rows, 8), rows), :] = right
        squares = squares + jnp.sum((right * right).reshape(-1, 8, RANK), axis=0)
    squares_ref[...] = squares


def right_of(at, own, other, inverse, left_raw):
    return pl.pallas_call(
        right_kernel,
        out_shape=(
            jax.ShapeDtypeStruct((2 * own.shape[0], RANK), jnp.float32),
            jax.ShapeDtypeStruct((8, RANK), jnp.float32),
            jax.ShapeDtypeStruct(left_raw.shape, jnp.float32),
        ),
        in_specs=[SM] + [VM] * 4,
        out_specs=(VM, VM, VM),
        compiler_params=params(),
        name="right",
    )(at, own, other, inverse, left_raw)


def update_kernel(
    decay, gain, right_ref, left_ref, buffer_ref, weight_ref, weight_out, momentum_out, factor_out,
    weight_new, momentum_new, factor_new, sent,
):
    near, pitch, _ = right_ref.shape
    chunk, group = pitch - 8, 2
    squares = right_ref[0, chunk:, :]
    for k in range(1, near):
        squares = squares + right_ref[k, chunk:, :]
    scale = lax.rsqrt(jnp.sum(squares, axis=0, keepdims=True) + 1e-06)
    left = left_ref[...]
    high, low = split(jnp.concatenate([decay * left, (gain * left) * scale], axis=0))
    both_left = jnp.concatenate(
        [
            jnp.concatenate([high, high], axis=1),
            jnp.concatenate([low, jnp.zeros_like(low)], axis=1),
        ],
        axis=0,
    )
    n = left.shape[0]
    copies = []

    def send(source, target):
        copies.append(pltpu.make_async_copy(source, target, sent.at[len(copies)]))
        copies[-1].start()

    for first in range(0, near, group):
        for k in range(first, first + group):
            factor_new[k * chunk : (k + 1) * chunk, :] = right_ref[k, :chunk, :] * scale
        at, end = first * chunk, (first + group) * chunk
        send(factor_new.at[at:end, :], factor_out.at[at:end, :])
    for first in range(0, near, group):
        at, end = first * chunk, (first + group) * chunk
        right = jnp.concatenate([right_ref[first + k, :chunk, :] for k in range(group)], axis=0)
        both = jnp.concatenate(split(right), axis=1)
        out = lax.dot_general(both_left, both, NT, preferred_element_type=jnp.float32)
        out = out[: 2 * n] + out[2 * n :]
        momentum_new[:, at:end] = buffer_ref[:, at:end] - out[:n]
        weight_new[:, at:end] = weight_ref[:, at:end] - out[n:]
        send(momentum_new.at[:, at:end], momentum_out.at[:, at:end])
        send(weight_new.at[:, at:end], weight_out.at[:, at:end])
    for copy in copies:
        copy.wait()


def update(decay, gain, right, left, buffer, weight):
    shapes = (weight.shape, weight.shape, (weight.shape[1], RANK))
    return pl.pallas_call(
        functools.partial(update_kernel, decay, gain),
        out_shape=tuple(jax.ShapeDtypeStruct(shape, jnp.float32) for shape in shapes),
        in_specs=[VM] * 4,
        out_specs=(ANY,) * 3,
        scratch_shapes=[pltpu.VMEM(shape, jnp.float32) for shape in shapes]
        + [pltpu.SemaphoreType.DMA((12,))],
        compiler_params=params(),
        name="update",
    )(right, left, buffer, weight)


def groups(same, order):
    found = {}
    for device in range(X * Y * Z * 2):
        chip, core = divmod(device, 2)
        x, y, z = shifted(chip, core)
        found.setdefault((core, same(x, y, z)), []).append((order(x, y, z), device))
    return [[device for _, device in sorted(members)] for members in found.values()]


def shifted(chip, core):
    return (chip // (Y * Z) + core) % X, (chip // Z % Y + core) % Y, (chip % Z + core) % Z


def cube(x, y, z):
    return x % 2, y % 2, z % 2


def far(x, y, z):
    return y // 2, z // 2


CUBE = groups(lambda x, y, z: (x // 2, y // 2, z // 2), cube)
NEAR = groups(far, lambda x, y, z: cube(x, y, z) + (x // 2,))
FAR = groups(lambda x, y, z: cube(x, y, z) + (x // 2,), far)


def exchange(blocks, members):
    return lax.all_to_all(blocks, ALL, 0, 0, axis_index_groups=members, tiled=True)


def gather(block, members):
    return exchange(jnp.broadcast_to(block[None], (len(members[0]),) + block.shape), members)


def per_device(weight, momentum, grad, right_factor):
    rows, cols = momentum.shape
    n_near, n_far = len(NEAR[0]), len(FAR[0])
    chunk = cols // n_near
    wide = -(-chunk // RANK) * RANK
    piece = chunk // n_far

    buffer = momentum + grad.astype(jnp.float32)
    parts, left_part = head(buffer, right_factor, n_near, wide)
    left_raw = lax.psum(left_part, "tensor")
    beside = jnp.broadcast_to(left_raw[None], (n_near, rows, RANK))
    held = exchange(jnp.concatenate([parts, beside], axis=2), NEAR)

    sent = part_of(held.reshape(n_near * rows, wide + RANK), n_far, piece)
    summed = jnp.sum(exchange(sent, FAR), axis=0)

    by_far = gather(summed, FAR)
    own = by_far[:, :piece].reshape(chunk, RANK)
    count = X * Y * Z
    other = lax.ppermute(own, "dp", [(i, (i + count // 2) % count) for i in range(count)])
    inverse = factor(by_far[:, piece:].reshape(-1, RANK))
    x = (lax.axis_index("dp") // (Y * Z) + lax.axis_index("tensor")) % X
    right, squares, left = right_of((x // 2).reshape(1), own, other, inverse, left_raw)
    squares = lax.psum(squares, "tensor")
    by_cube = gather(jnp.concatenate([right, squares], axis=0), CUBE)
    gain = 0.5 * math.sqrt(count * rows * 2 * cols / RANK)
    return update(1.0 - 0.95, gain, by_cube, left, buffer, weight)


def solution(mesh):
    in_specs = (P("dp", "tensor"), P("dp", "tensor"), P("dp", "tensor"), P("tensor", None))
    out_specs = (P("dp", "tensor"), P("dp", "tensor"), P("tensor", None))
    return jax.shard_map(
        per_device, mesh=mesh, in_specs=in_specs, out_specs=out_specs, check_vma=False
    )
```

```python
import functools
import math

import jax
import jax.numpy as jnp
from jax import lax
from jax.experimental import pallas as pl
from jax.experimental.pallas import tpu as pltpu
from jax.sharding import PartitionSpec as P

PRECISE = lax.Precision.HIGHEST
X, Y, Z = 4, 8, 12
ALL = ("dp", "tensor")
RANK = 128
NT = (((1,), (1,)), ((), ()))
TN = (((0,), (0,)), ((), ()))
VM = pl.BlockSpec(memory_space=pltpu.VMEM)
SM = pl.BlockSpec(memory_space=pltpu.SMEM)
ANY = pl.BlockSpec(memory_space=pl.ANY)


def params(limit=16 * 1024 * 1024):
    return pltpu.CompilerParams(vmem_limit_bytes=limit)


def split(value, parts=2):
    out = []
    for _ in range(parts):
        out.append(value.astype(jnp.bfloat16))
        value = value - out[-1].astype(jnp.float32)
    return out


def head_kernel(buffer_ref, factor_ref, parts_ref, left_ref, held, arrived):
    n_parts, rows, wide = parts_ref.shape
    cols = buffer_ref.shape[1]
    chunk, third = cols // n_parts, cols // 3
    copies = [
        pltpu.make_async_copy(
            factor_ref.at[at : at + third, :], held.at[at : at + third, :], arrived.at[k]
        )
        for k, at in enumerate(range(0, cols, third))
    ]
    for copy in copies:
        copy.start()
    zeros = jnp.zeros((rows, wide - chunk), jnp.float32)
    for k in range(n_parts):
        part = buffer_ref[:, k * chunk : (k + 1) * chunk]
        parts_ref[k, :, :] = jnp.concatenate([part, zeros], axis=1)
    total = jnp.zeros((rows, RANK), jnp.float32)
    for k, copy in enumerate(copies):
        copy.wait()
        b1, b2 = split(buffer_ref[:, k * third : (k + 1) * third])
        f1, f2 = split(held[k * third : (k + 1) * third, :])
        both = jnp.dot(jnp.concatenate([b1, b2], axis=0), f1, preferred_element_type=jnp.float32)
        small = both[rows:] + jnp.dot(b1, f2, preferred_element_type=jnp.float32)
        total = total + (small + both[:rows])
    left_ref[...] = total


def head(buffer, right_factor, n_parts, wide):
    rows = buffer.shape[0]
    return pl.pallas_call(
        head_kernel,
        out_shape=(
            jax.ShapeDtypeStruct((n_parts, rows, wide), jnp.float32),
            jax.ShapeDtypeStruct((rows, RANK), jnp.float32),
        ),
        in_specs=[VM, ANY],
        out_specs=(VM, VM),
        scratch_shapes=[
            pltpu.VMEM(right_factor.shape, jnp.float32),
            pltpu.SemaphoreType.DMA((3,)),
        ],
        compiler_params=params(54_000_000),
        name="head",
    )(buffer, right_factor)


def part_kernel(piece, held_ref, sent_ref, part):
    n, pitch, _ = sent_ref.shape
    wide, share, half = held_ref.shape[1] - RANK, pitch - piece, RANK // 2
    h1, h2 = split(held_ref[...])
    l1, l2 = h1[:, wide:], h2[:, wide:]
    product = lax.dot_general(
        jnp.concatenate([h2, h1, h1], axis=0),
        jnp.concatenate([l1, l2, l1], axis=0),
        TN,
        preferred_element_type=jnp.float32,
    )
    part[...] = product[: n * piece]
    corner = product[wide + half :, half:]
    corner = jnp.concatenate([corner[: half // 2], corner[half // 2 :]], axis=1)
    packed = jnp.concatenate([product[wide : wide + half], corner], axis=0)
    for k in range(n):
        sent_ref[k, :piece, :] = part[k * piece : (k + 1) * piece, :]
        sent_ref[k, piece:, :] = packed[k * share : (k + 1) * share, :]


def part_of(held, n, piece):
    share = (RANK // 2 + RANK // 4) // n
    return pl.pallas_call(
        functools.partial(part_kernel, piece),
        out_shape=jax.ShapeDtypeStruct((n, piece + share, RANK), jnp.float32),
        in_specs=[VM],
        out_specs=VM,
        scratch_shapes=[pltpu.VMEM((n * piece, RANK), jnp.float32)],
        compiler_params=params(),
        name="part",
    )(held)


def inverse_factor(gram, store):
    step = 16
    row = lax.broadcasted_iota(jnp.int32, (RANK, RANK), 0)
    col = lax.broadcasted_iota(jnp.int32, (RANK, RANK), 1)
    rest = jnp.concatenate([gram, (row == col).astype(jnp.float32)], axis=1)
    for at in range(0, RANK, step):
        rows = [rest[i : i + 1, :] for i in range(step)]
        corner = rest[:step, at : at + step]
        entry = {
            (i, j): jnp.broadcast_to(corner[i : i + 1, j : j + 1], (1, RANK))
            for i in range(step)
            for j in range(i, step)
        }
        for i in range(step):
            scale = lax.rsqrt(entry[i, i])
            pivot = {j: entry[i, j] * scale for j in range(i + 1, step)}
            rows[i] = rows[i] * jnp.concatenate([scale, scale], axis=1)
            for j in range(i + 1, step):
                rows[j] = rows[j] - jnp.concatenate([pivot[j], pivot[j]], axis=1) * rows[i]
                for k in range(j, step):
                    entry[j, k] = entry[j, k] - pivot[j] * pivot[k]
        done = jnp.concatenate(rows, axis=0)
        store(at, done[:, RANK:])
        if at + step < RANK:
            l1, l2, l3 = split(done[:, :RANK], 3)
            r1, r2, r3 = split(done, 3)
            change = lax.dot_general(
                jnp.concatenate([l1, l1, l2, l2, l1, l3], axis=0),
                jnp.concatenate([r1, r2, r1, r2, r3, r1], axis=0),
                TN,
                preferred_element_type=jnp.float32,
            )
            rest = rest[step:] - change[at + step :]


def factor_kernel(packed_ref, inverse_ref):
    half = RANK // 2
    rest = packed_ref[half:, :]
    nothing = jnp.zeros((half // 2, half), jnp.float32)
    gram = jnp.concatenate(
        [
            packed_ref[:half, :],
            jnp.concatenate([nothing, rest[:, :half]], axis=1),
            jnp.concatenate([nothing, rest[:, half:]], axis=1),
        ],
        axis=0,
    )

    def store(at, rows):
        inverse_ref[at : at + rows.shape[0], :] = rows

    inverse_factor(gram, store)


def factor(packed_gram):
    return pl.pallas_call(
        factor_kernel,
        out_shape=jax.ShapeDtypeStruct((RANK, RANK), jnp.float32),
        in_specs=[VM],
        out_specs=VM,
        compiler_params=params(),
        name="factor",
    )(packed_gram)


def right_kernel(at_ref, own_ref, other_ref, inverse_ref, left_raw_ref, right_ref, squares_ref, left_ref):
    rows = own_ref.shape[0]
    inverse = inverse_ref[...]
    left_ref[...] = lax.dot_general(
        left_raw_ref[...], inverse, NT, precision=PRECISE, preferred_element_type=jnp.float32
    )
    squares = jnp.zeros((8, RANK), jnp.float32)
    for place, raw in ((at_ref[0], own_ref), (1 - at_ref[0], other_ref)):
        right = lax.dot_general(
            raw[...], inverse, NT, precision=PRECISE, preferred_element_type=jnp.float32
        )
        right_ref[pl.ds(pl.multiple_of(place * rows, 8), rows), :] = right
        squares = squares + jnp.sum((right * right).reshape(-1, 8, RANK), axis=0)
    squares_ref[...] = squares


def right_of(at, own, other, inverse, left_raw):
    return pl.pallas_call(
        right_kernel,
        out_shape=(
            jax.ShapeDtypeStruct((2 * own.shape[0], RANK), jnp.float32),
            jax.ShapeDtypeStruct((8, RANK), jnp.float32),
            jax.ShapeDtypeStruct(left_raw.shape, jnp.float32),
        ),
        in_specs=[SM] + [VM] * 4,
        out_specs=(VM, VM, VM),
        compiler_params=params(),
        name="right",
    )(at, own, other, inverse, left_raw)


def update_kernel(
    decay, gain, right_ref, left_ref, buffer_ref, weight_ref, weight_out, momentum_out, factor_out,
    weight_new, momentum_new, factor_new, sent,
):
    near, pitch, _ = right_ref.shape
    chunk, group = pitch - 8, 2
    squares = right_ref[0, chunk:, :]
    for k in range(1, near):
        squares = squares + right_ref[k, chunk:, :]
    scale = lax.rsqrt(jnp.sum(squares, axis=0, keepdims=True) + 1e-06)
    left = left_ref[...]
    high, low = split(jnp.concatenate([decay * left, (gain * left) * scale], axis=0))
    both_left = jnp.concatenate(
        [
            jnp.concatenate([high, high], axis=1),
            jnp.concatenate([low, jnp.zeros_like(low)], axis=1),
        ],
        axis=0,
    )
    n = left.shape[0]
    copies = []

    def send(source, target):
        copies.append(pltpu.make_async_copy(source, target, sent.at[len(copies)]))
        copies[-1].start()

    for first in range(0, near, group):
        for k in range(first, first + group):
            factor_new[k * chunk : (k + 1) * chunk, :] = right_ref[k, :chunk, :] * scale
        at, end = first * chunk, (first + group) * chunk
        send(factor_new.at[at:end, :], factor_out.at[at:end, :])
    for first in range(0, near, group):
        at, end = first * chunk, (first + group) * chunk
        right = jnp.concatenate([right_ref[first + k, :chunk, :] for k in range(group)], axis=0)
        both = jnp.concatenate(split(right), axis=1)
        out = lax.dot_general(both_left, both, NT, preferred_element_type=jnp.float32)
        out = out[: 2 * n] + out[2 * n :]
        momentum_new[:, at:end] = buffer_ref[:, at:end] - out[:n]
        weight_new[:, at:end] = weight_ref[:, at:end] - out[n:]
        send(momentum_new.at[:, at:end], momentum_out.at[:, at:end])
        send(weight_new.at[:, at:end], weight_out.at[:, at:end])
    for copy in copies:
        copy.wait()


def update(decay, gain, right, left, buffer, weight):
    shapes = (weight.shape, weight.shape, (weight.shape[1], RANK))
    return pl.pallas_call(
        functools.partial(update_kernel, decay, gain),
        out_shape=tuple(jax.ShapeDtypeStruct(shape, jnp.float32) for shape in shapes),
        in_specs=[VM] * 4,
        out_specs=(ANY,) * 3,
        scratch_shapes=[pltpu.VMEM(shape, jnp.float32) for shape in shapes]
        + [pltpu.SemaphoreType.DMA((12,))],
        compiler_params=params(),
        name="update",
    )(right, left, buffer, weight)


def groups(same, order):
    found = {}
    for device in range(X * Y * Z * 2):
        chip, core = divmod(device, 2)
        x, y, z = shifted(chip, core)
        found.setdefault((core, same(x, y, z)), []).append((order(x, y, z), device))
    return [[device for _, device in sorted(members)] for members in found.values()]


def shifted(chip, core):
    return (chip // (Y * Z) + core) % X, (chip // Z % Y + core) % Y, (chip % Z + core) % Z


def cube(x, y, z):
    return x % 2, y % 2, z % 2


def far(x, y, z):
    return y // 2, z // 2


CUBE = groups(lambda x, y, z: (x // 2, y // 2, z // 2), cube)
NEAR = groups(far, lambda x, y, z: cube(x, y, z) + (x // 2,))
FAR = groups(lambda x, y, z: cube(x, y, z) + (x // 2,), far)


def exchange(blocks, members):
    return lax.all_to_all(blocks, ALL, 0, 0, axis_index_groups=members, tiled=True)


def gather(block, members):
    return exchange(jnp.broadcast_to(block[None], (len(members[0]),) + block.shape), members)


def per_device(weight, momentum, grad, right_factor):
    rows, cols = momentum.shape
    n_near, n_far = len(NEAR[0]), len(FAR[0])
    chunk = cols // n_near
    wide = -(-chunk // RANK) * RANK
    piece = chunk // n_far

    buffer = momentum + grad.astype(jnp.float32)
    parts, left_part = head(buffer, right_factor, n_near, wide)
    left_raw = lax.psum(left_part, "tensor")
    beside = jnp.broadcast_to(left_raw[None], (n_near, rows, RANK))
    held = exchange(jnp.concatenate([parts, beside], axis=2), NEAR)

    sent = part_of(held.reshape(n_near * rows, wide + RANK), n_far, piece)
    summed = jnp.sum(exchange(sent, FAR), axis=0)

    by_far = gather(summed, FAR)
    own = by_far[:, :piece].reshape(chunk, RANK)
    count = X * Y * Z
    other = lax.ppermute(own, "dp", [(i, (i + count // 2) % count) for i in range(count)])
    inverse = factor(by_far[:, piece:].reshape(-1, RANK))
    x = (lax.axis_index("dp") // (Y * Z) + lax.axis_index("tensor")) % X
    right, squares, left = right_of((x // 2).reshape(1), own, other, inverse, left_raw)
    squares = lax.psum(squares, "tensor")
    by_cube = gather(jnp.concatenate([right, squares], axis=0), CUBE)
    gain = 0.5 * math.sqrt(count * rows * 2 * cols / RANK)
    return update(1.0 - 0.95, gain, by_cube, left, buffer, weight)


def solution(mesh):
    in_specs = (P("dp", "tensor"), P("dp", "tensor"), P("dp", "tensor"), P("tensor", None))
    out_specs = (P("dp", "tensor"), P("dp", "tensor"), P("tensor", None))
    return jax.shard_map(
        per_device, mesh=mesh, in_specs=in_specs, out_specs=out_specs, check_vma=False
    )
```

```python
import functools
import math

import jax
import jax.numpy as jnp
from jax import lax
from jax.experimental import pallas as pl
from jax.experimental.pallas import tpu as pltpu
from jax.sharding import PartitionSpec as P

PRECISE = lax.Precision.HIGHEST
X, Y, Z = 4, 8, 12
ALL = ("dp", "tensor")
RANK = 128
NT = (((1,), (1,)), ((), ()))
TN = (((0,), (0,)), ((), ()))
VM = pl.BlockSpec(memory_space=pltpu.VMEM)
SM = pl.BlockSpec(memory_space=pltpu.SMEM)
ANY = pl.BlockSpec(memory_space=pl.ANY)


def params(limit=16 * 1024 * 1024):
    return pltpu.CompilerParams(vmem_limit_bytes=limit)


def split(value, parts=2):
    out = []
    for _ in range(parts):
        out.append(value.astype(jnp.bfloat16))
        value = value - out[-1].astype(jnp.float32)
    return out


def head_kernel(buffer_ref, factor_ref, parts_ref, left_ref, held, arrived):
    n_parts, rows, wide = parts_ref.shape
    cols = buffer_ref.shape[1]
    chunk, third = cols // n_parts, cols // 3
    copies = [
        pltpu.make_async_copy(
            factor_ref.at[at : at + third, :], held.at[at : at + third, :], arrived.at[k]
        )
        for k, at in enumerate(range(0, cols, third))
    ]
    for copy in copies:
        copy.start()
    zeros = jnp.zeros((rows, wide - chunk), jnp.float32)
    for k in range(n_parts):
        part = buffer_ref[:, k * chunk : (k + 1) * chunk]
        parts_ref[k, :, :] = jnp.concatenate([part, zeros], axis=1)
    total = jnp.zeros((rows, RANK), jnp.float32)
    for k, copy in enumerate(copies):
        copy.wait()
        b1, b2 = split(buffer_ref[:, k * third : (k + 1) * third])
        f1, f2 = split(held[k * third : (k + 1) * third, :])
        both = jnp.dot(jnp.concatenate([b1, b2], axis=0), f1, preferred_element_type=jnp.float32)
        small = both[rows:] + jnp.dot(b1, f2, preferred_element_type=jnp.float32)
        total = total + (small + both[:rows])
    left_ref[...] = total


def head(buffer, right_factor, n_parts, wide):
    rows = buffer.shape[0]
    return pl.pallas_call(
        head_kernel,
        out_shape=(
            jax.ShapeDtypeStruct((n_parts, rows, wide), jnp.float32),
            jax.ShapeDtypeStruct((rows, RANK), jnp.float32),
        ),
        in_specs=[VM, ANY],
        out_specs=(VM, VM),
        scratch_shapes=[
            pltpu.VMEM(right_factor.shape, jnp.float32),
            pltpu.SemaphoreType.DMA((3,)),
        ],
        compiler_params=params(54_000_000),
        name="head",
    )(buffer, right_factor)


def part_kernel(piece, held_ref, sent_ref, part):
    n, pitch, _ = sent_ref.shape
    wide, share, half = held_ref.shape[1] - RANK, pitch - piece, RANK // 2
    h1, h2 = split(held_ref[...])
    l1, l2 = h1[:, wide:], h2[:, wide:]
    product = lax.dot_general(
        jnp.concatenate([h2, h1, h1], axis=0),
        jnp.concatenate([l1, l2, l1], axis=0),
        TN,
        preferred_element_type=jnp.float32,
    )
    part[...] = product[: n * piece]
    corner = product[wide + half :, half:]
    corner = jnp.concatenate([corner[: half // 2], corner[half // 2 :]], axis=1)
    packed = jnp.concatenate([product[wide : wide + half], corner], axis=0)
    for k in range(n):
        sent_ref[k, :piece, :] = part[k * piece : (k + 1) * piece, :]
        sent_ref[k, piece:, :] = packed[k * share : (k + 1) * share, :]


def part_of(held, n, piece):
    share = (RANK // 2 + RANK // 4) // n
    return pl.pallas_call(
        functools.partial(part_kernel, piece),
        out_shape=jax.ShapeDtypeStruct((n, piece + share, RANK), jnp.float32),
        in_specs=[VM],
        out_specs=VM,
        scratch_shapes=[pltpu.VMEM((n * piece, RANK), jnp.float32)],
        compiler_params=params(),
        name="part",
    )(held)


def inverse_factor(gram, store):
    step = 16
    row = lax.broadcasted_iota(jnp.int32, (RANK, RANK), 0)
    col = lax.broadcasted_iota(jnp.int32, (RANK, RANK), 1)
    rest = jnp.concatenate([gram, (row == col).astype(jnp.float32)], axis=1)
    for at in range(0, RANK, step):
        rows = [rest[i : i + 1, :] for i in range(step)]
        corner = rest[:step, at : at + step]
        entry = {
            (i, j): jnp.broadcast_to(corner[i : i + 1, j : j + 1], (1, RANK))
            for i in range(step)
            for j in range(i, step)
        }
        for i in range(step):
            scale = lax.rsqrt(entry[i, i])
            pivot = {j: entry[i, j] * scale for j in range(i + 1, step)}
            rows[i] = rows[i] * jnp.concatenate([scale, scale], axis=1)
            for j in range(i + 1, step):
                rows[j] = rows[j] - jnp.concatenate([pivot[j], pivot[j]], axis=1) * rows[i]
                for k in range(j, step):
                    entry[j, k] = entry[j, k] - pivot[j] * pivot[k]
        done = jnp.concatenate(rows, axis=0)
        store(at, done[:, RANK:])
        if at + step < RANK:
            l1, l2, l3 = split(done[:, :RANK], 3)
            r1, r2, r3 = split(done, 3)
            change = lax.dot_general(
                jnp.concatenate([l1, l1, l2, l2, l1, l3], axis=0),
                jnp.concatenate([r1, r2, r1, r2, r3, r1], axis=0),
                TN,
                preferred_element_type=jnp.float32,
            )
            rest = rest[step:] - change[at + step :]


def factor_kernel(packed_ref, inverse_ref):
    half = RANK // 2
    rest = packed_ref[half:, :]
    nothing = jnp.zeros((half // 2, half), jnp.float32)
    gram = jnp.concatenate(
        [
            packed_ref[:half, :],
            jnp.concatenate([nothing, rest[:, :half]], axis=1),
            jnp.concatenate([nothing, rest[:, half:]], axis=1),
        ],
        axis=0,
    )

    def store(at, rows):
        inverse_ref[at : at + rows.shape[0], :] = rows

    inverse_factor(gram, store)


def factor(packed_gram):
    return pl.pallas_call(
        factor_kernel,
        out_shape=jax.ShapeDtypeStruct((RANK, RANK), jnp.float32),
        in_specs=[VM],
        out_specs=VM,
        compiler_params=params(),
        name="factor",
    )(packed_gram)


def right_kernel(at_ref, own_ref, other_ref, inverse_ref, left_raw_ref, right_ref, squares_ref, left_ref):
    rows = own_ref.shape[0]
    inverse = inverse_ref[...]
    left_ref[...] = lax.dot_general(
        left_raw_ref[...], inverse, NT, precision=PRECISE, preferred_element_type=jnp.float32
    )
    squares = jnp.zeros((8, RANK), jnp.float32)
    for place, raw in ((at_ref[0], own_ref), (1 - at_ref[0], other_ref)):
        right = lax.dot_general(
            raw[...], inverse, NT, precision=PRECISE, preferred_element_type=jnp.float32
        )
        right_ref[pl.ds(pl.multiple_of(place * rows, 8), rows), :] = right
        squares = squares + jnp.sum((right * right).reshape(-1, 8, RANK), axis=0)
    squares_ref[...] = squares


def right_of(at, own, other, inverse, left_raw):
    return pl.pallas_call(
        right_kernel,
        out_shape=(
            jax.ShapeDtypeStruct((2 * own.shape[0], RANK), jnp.float32),
            jax.ShapeDtypeStruct((8, RANK), jnp.float32),
            jax.ShapeDtypeStruct(left_raw.shape, jnp.float32),
        ),
        in_specs=[SM] + [VM] * 4,
        out_specs=(VM, VM, VM),
        compiler_params=params(),
        name="right",
    )(at, own, other, inverse, left_raw)


def update_kernel(
    decay, gain, right_ref, left_ref, buffer_ref, weight_ref, weight_out, momentum_out, factor_out,
    weight_new, momentum_new, factor_new, sent,
):
    near, pitch, _ = right_ref.shape
    chunk, group = (pitch - 8) // 2, 4
    squares = right_ref[0, 2 * chunk :, :]
    for k in range(1, near):
        squares = squares + right_ref[k, 2 * chunk :, :]
    scale = lax.rsqrt(jnp.sum(squares, axis=0, keepdims=True) + 1e-06)
    left = left_ref[...]
    high, low = split(jnp.concatenate([decay * left, (gain * left) * scale], axis=0))
    both_left = jnp.concatenate(
        [
            jnp.concatenate([high, high], axis=1),
            jnp.concatenate([low, jnp.zeros_like(low)], axis=1),
        ],
        axis=0,
    )
    n = left.shape[0]
    copies = []

    def send(source, target):
        copies.append(pltpu.make_async_copy(source, target, sent.at[len(copies)]))
        copies[-1].start()

    blocks = [(half, first) for half in range(2) for first in range(0, near, group)]
    for half, first in blocks:
        at = (half * near + first) * chunk
        end = at + group * chunk
        for k in range(group):
            rows = right_ref[first + k, half * chunk : (half + 1) * chunk, :]
            factor_new[at + k * chunk : at + (k + 1) * chunk, :] = rows * scale
        send(factor_new.at[at:end, :], factor_out.at[at:end, :])
    for half, first in blocks:
        at = (half * near + first) * chunk
        end = at + group * chunk
        right = jnp.concatenate(
            [right_ref[first + k, half * chunk : (half + 1) * chunk, :] for k in range(group)], axis=0
        )
        both = jnp.concatenate(split(right), axis=1)
        out = lax.dot_general(both_left, both, NT, preferred_element_type=jnp.float32)
        out = out[: 2 * n] + out[2 * n :]
        momentum_new[:, at:end] = buffer_ref[:, at:end] - out[:n]
        weight_new[:, at:end] = weight_ref[:, at:end] - out[n:]
        send(momentum_new.at[:, at:end], momentum_out.at[:, at:end])
        send(weight_new.at[:, at:end], weight_out.at[:, at:end])
    for copy in copies:
        copy.wait()


def update(decay, gain, right, left, buffer, weight):
    shapes = (weight.shape, weight.shape, (weight.shape[1], RANK))
    return pl.pallas_call(
        functools.partial(update_kernel, decay, gain),
        out_shape=tuple(jax.ShapeDtypeStruct(shape, jnp.float32) for shape in shapes),
        in_specs=[VM] * 4,
        out_specs=(ANY,) * 3,
        scratch_shapes=[pltpu.VMEM(shape, jnp.float32) for shape in shapes]
        + [pltpu.SemaphoreType.DMA((12,))],
        compiler_params=params(),
        name="update",
    )(right, left, buffer, weight)


def groups(same, order):
    found = {}
    for device in range(X * Y * Z * 2):
        chip, core = divmod(device, 2)
        x, y, z = shifted(chip, core)
        found.setdefault((core, same(x, y, z)), []).append((order(x, y, z), device))
    return [[device for _, device in sorted(members)] for members in found.values()]


def shifted(chip, core):
    return (chip // (Y * Z) + core) % X, (chip // Z % Y + core) % Y, (chip % Z + core) % Z


def cube(x, y, z):
    return x % 2, y % 2, z % 2


def far(x, y, z):
    return z // 2, y // 2


CUBE = groups(lambda x, y, z: (x // 2, y // 2, z // 2), cube)
NEAR = groups(far, lambda x, y, z: (x // 2,) + cube(x, y, z))
FAR = groups(lambda x, y, z: cube(x, y, z) + (x // 2,), far)


def exchange(blocks, members):
    return lax.all_to_all(blocks, ALL, 0, 0, axis_index_groups=members, tiled=True)


def gather(block, members):
    return exchange(jnp.broadcast_to(block[None], (len(members[0]),) + block.shape), members)


def per_device(weight, momentum, grad, right_factor):
    rows, cols = momentum.shape
    n_near, n_far = len(NEAR[0]), len(FAR[0])
    chunk = cols // n_near
    wide = -(-chunk // RANK) * RANK
    piece = chunk // n_far

    buffer = momentum + grad.astype(jnp.float32)
    parts, left_part = head(buffer, right_factor, n_near, wide)
    left_raw = lax.psum(left_part, "tensor")
    beside = jnp.broadcast_to(left_raw[None], (n_near, rows, RANK))
    held = exchange(jnp.concatenate([parts, beside], axis=2), NEAR)

    sent = part_of(held.reshape(n_near * rows, wide + RANK), n_far, piece)
    summed = jnp.sum(exchange(sent, FAR), axis=0)

    by_far = gather(summed, FAR)
    own = by_far[:, :piece].reshape(chunk, RANK)
    count = X * Y * Z
    other = lax.ppermute(own, "dp", [(i, (i + count // 2) % count) for i in range(count)])
    inverse = factor(by_far[:, piece:].reshape(-1, RANK))
    x = (lax.axis_index("dp") // (Y * Z) + lax.axis_index("tensor")) % X
    right, squares, left = right_of((x // 2).reshape(1), own, other, inverse, left_raw)
    squares = lax.psum(squares, "tensor")
    by_cube = gather(jnp.concatenate([right, squares], axis=0), CUBE)
    gain = 0.5 * math.sqrt(count * rows * 2 * cols / RANK)
    return update(1.0 - 0.95, gain, by_cube, left, buffer, weight)


def solution(mesh):
    in_specs = (P("dp", "tensor"), P("dp", "tensor"), P("dp", "tensor"), P("tensor", None))
    out_specs = (P("dp", "tensor"), P("dp", "tensor"), P("tensor", None))
    return jax.shard_map(
        per_device, mesh=mesh, in_specs=in_specs, out_specs=out_specs, check_vma=False
    )
```

```python
import functools
import math

import jax
import jax.numpy as jnp
from jax import lax
from jax.experimental import pallas as pl
from jax.experimental.pallas import tpu as pltpu
from jax.sharding import PartitionSpec as P

PRECISE = lax.Precision.HIGHEST
X, Y, Z = 4, 8, 12
ALL = ("dp", "tensor")
RANK = 128
NT = (((1,), (1,)), ((), ()))
TN = (((0,), (0,)), ((), ()))
VM = pl.BlockSpec(memory_space=pltpu.VMEM)
SM = pl.BlockSpec(memory_space=pltpu.SMEM)
ANY = pl.BlockSpec(memory_space=pl.ANY)


def params(limit=16 * 1024 * 1024):
    return pltpu.CompilerParams(vmem_limit_bytes=limit)


def split(value, parts=2):
    out = []
    for _ in range(parts):
        out.append(value.astype(jnp.bfloat16))
        value = value - out[-1].astype(jnp.float32)
    return out


def head_kernel(buffer_ref, factor_ref, parts_ref, left_ref, held, arrived):
    n_parts, rows, wide = parts_ref.shape
    cols = buffer_ref.shape[1]
    chunk, third = cols // n_parts, cols // 3
    copies = [
        pltpu.make_async_copy(
            factor_ref.at[at : at + third, :], held.at[at : at + third, :], arrived.at[k]
        )
        for k, at in enumerate(range(0, cols, third))
    ]
    for copy in copies:
        copy.start()
    zeros = jnp.zeros((rows, wide - chunk), jnp.float32)
    for k in range(n_parts):
        part = buffer_ref[:, k * chunk : (k + 1) * chunk]
        parts_ref[k, :, :] = jnp.concatenate([part, zeros], axis=1)
    total = jnp.zeros((rows, RANK), jnp.float32)
    for k, copy in enumerate(copies):
        copy.wait()
        b1, b2 = split(buffer_ref[:, k * third : (k + 1) * third])
        f1, f2 = split(held[k * third : (k + 1) * third, :])
        both = jnp.dot(jnp.concatenate([b1, b2], axis=0), f1, preferred_element_type=jnp.float32)
        small = both[rows:] + jnp.dot(b1, f2, preferred_element_type=jnp.float32)
        total = total + (small + both[:rows])
    left_ref[...] = total


def head(buffer, right_factor, n_parts, wide):
    rows = buffer.shape[0]
    return pl.pallas_call(
        head_kernel,
        out_shape=(
            jax.ShapeDtypeStruct((n_parts, rows, wide), jnp.float32),
            jax.ShapeDtypeStruct((rows, RANK), jnp.float32),
        ),
        in_specs=[VM, ANY],
        out_specs=(VM, VM),
        scratch_shapes=[
            pltpu.VMEM(right_factor.shape, jnp.float32),
            pltpu.SemaphoreType.DMA((3,)),
        ],
        compiler_params=params(54_000_000),
        name="head",
    )(buffer, right_factor)


def part_kernel(piece, held_ref, sent_ref, part):
    n, pitch, _ = sent_ref.shape
    wide, share, half = held_ref.shape[1] - RANK, pitch - piece, RANK // 2
    h1, h2 = split(held_ref[...])
    l1, l2 = h1[:, wide:], h2[:, wide:]
    product = lax.dot_general(
        jnp.concatenate([h2, h1, h1], axis=0),
        jnp.concatenate([l1, l2, l1], axis=0),
        TN,
        preferred_element_type=jnp.float32,
    )
    part[...] = product[: n * piece]
    corner = product[wide + half :, half:]
    corner = jnp.concatenate([corner[: half // 2], corner[half // 2 :]], axis=1)
    packed = jnp.concatenate([product[wide : wide + half], corner], axis=0)
    for k in range(n):
        sent_ref[k, :piece, :] = part[k * piece : (k + 1) * piece, :]
        sent_ref[k, piece:, :] = packed[k * share : (k + 1) * share, :]


def part_of(held, n, piece):
    share = (RANK // 2 + RANK // 4) // n
    return pl.pallas_call(
        functools.partial(part_kernel, piece),
        out_shape=jax.ShapeDtypeStruct((n, piece + share, RANK), jnp.float32),
        in_specs=[VM],
        out_specs=VM,
        scratch_shapes=[pltpu.VMEM((n * piece, RANK), jnp.float32)],
        compiler_params=params(),
        name="part",
    )(held)


def inverse_factor(gram, store):
    step = 16
    row = lax.broadcasted_iota(jnp.int32, (RANK, RANK), 0)
    col = lax.broadcasted_iota(jnp.int32, (RANK, RANK), 1)
    rest = jnp.concatenate([gram, (row == col).astype(jnp.float32)], axis=1)
    for at in range(0, RANK, step):
        rows = [rest[i : i + 1, :] for i in range(step)]
        corner = rest[:step, at : at + step]
        entry = {
            (i, j): jnp.broadcast_to(corner[i : i + 1, j : j + 1], (1, RANK))
            for i in range(step)
            for j in range(i, step)
        }
        for i in range(step):
            scale = lax.rsqrt(entry[i, i])
            pivot = {j: entry[i, j] * scale for j in range(i + 1, step)}
            rows[i] = rows[i] * jnp.concatenate([scale, scale], axis=1)
            for j in range(i + 1, step):
                rows[j] = rows[j] - jnp.concatenate([pivot[j], pivot[j]], axis=1) * rows[i]
                for k in range(j, step):
                    entry[j, k] = entry[j, k] - pivot[j] * pivot[k]
        done = jnp.concatenate(rows, axis=0)
        store(at, done[:, RANK:])
        if at + step < RANK:
            l1, l2, l3 = split(done[:, :RANK], 3)
            r1, r2, r3 = split(done, 3)
            change = lax.dot_general(
                jnp.concatenate([l1, l1, l2, l2, l1, l3], axis=0),
                jnp.concatenate([r1, r2, r1, r2, r3, r1], axis=0),
                TN,
                preferred_element_type=jnp.float32,
            )
            rest = rest[step:] - change[at + step :]


def factor_kernel(packed_ref, inverse_ref):
    half = RANK // 2
    rest = packed_ref[half:, :]
    nothing = jnp.zeros((half // 2, half), jnp.float32)
    gram = jnp.concatenate(
        [
            packed_ref[:half, :],
            jnp.concatenate([nothing, rest[:, :half]], axis=1),
            jnp.concatenate([nothing, rest[:, half:]], axis=1),
        ],
        axis=0,
    )

    def store(at, rows):
        inverse_ref[at : at + rows.shape[0], :] = rows

    inverse_factor(gram, store)


def factor(packed_gram):
    return pl.pallas_call(
        factor_kernel,
        out_shape=jax.ShapeDtypeStruct((RANK, RANK), jnp.float32),
        in_specs=[VM],
        out_specs=VM,
        compiler_params=params(),
        name="factor",
    )(packed_gram)


def right_kernel(at_ref, own_ref, other_ref, inverse_ref, left_raw_ref, right_ref, squares_ref, left_ref):
    rows = own_ref.shape[0]
    inverse = inverse_ref[...]
    left_ref[...] = lax.dot_general(
        left_raw_ref[...], inverse, NT, precision=PRECISE, preferred_element_type=jnp.float32
    )
    squares = jnp.zeros((8, RANK), jnp.float32)
    for place, raw in ((at_ref[0], own_ref), (1 - at_ref[0], other_ref)):
        right = lax.dot_general(
            raw[...], inverse, NT, precision=PRECISE, preferred_element_type=jnp.float32
        )
        right_ref[pl.ds(pl.multiple_of(place * rows, 8), rows), :] = right
        squares = squares + jnp.sum((right * right).reshape(-1, 8, RANK), axis=0)
    squares_ref[...] = squares


def right_of(at, own, other, inverse, left_raw):
    return pl.pallas_call(
        right_kernel,
        out_shape=(
            jax.ShapeDtypeStruct((2 * own.shape[0], RANK), jnp.float32),
            jax.ShapeDtypeStruct((8, RANK), jnp.float32),
            jax.ShapeDtypeStruct(left_raw.shape, jnp.float32),
        ),
        in_specs=[SM] + [VM] * 4,
        out_specs=(VM, VM, VM),
        compiler_params=params(),
        name="right",
    )(at, own, other, inverse, left_raw)


def update_kernel(
    decay, gain, right_ref, left_ref, buffer_ref, weight_ref, weight_out, momentum_out, factor_out,
    weight_new, momentum_new, factor_new, sent,
):
    near, pitch, _ = right_ref.shape
    chunk, group = (pitch - 8) // 2, 4
    squares = right_ref[0, 2 * chunk :, :]
    for k in range(1, near):
        squares = squares + right_ref[k, 2 * chunk :, :]
    scale = lax.rsqrt(jnp.sum(squares, axis=0, keepdims=True) + 1e-06)
    left = left_ref[...]
    high, low = split(jnp.concatenate([decay * left, (gain * left) * scale], axis=0))
    both_left = jnp.concatenate(
        [
            jnp.concatenate([high, high], axis=1),
            jnp.concatenate([low, jnp.zeros_like(low)], axis=1),
        ],
        axis=0,
    )
    n = left.shape[0]
    copies = []

    def send(source, target):
        copies.append(pltpu.make_async_copy(source, target, sent.at[len(copies)]))
        copies[-1].start()

    blocks = [(half, first) for half in range(2) for first in range(0, near, group)]
    for half, first in blocks:
        at = (half * near + first) * chunk
        end = at + group * chunk
        for k in range(group):
            rows = right_ref[first + k, half * chunk : (half + 1) * chunk, :]
            factor_new[at + k * chunk : at + (k + 1) * chunk, :] = rows * scale
        send(factor_new.at[at:end, :], factor_out.at[at:end, :])
    for half, first in blocks:
        at = (half * near + first) * chunk
        end = at + group * chunk
        right = jnp.concatenate(
            [right_ref[first + k, half * chunk : (half + 1) * chunk, :] for k in range(group)], axis=0
        )
        both = jnp.concatenate(split(right), axis=1)
        out = lax.dot_general(both_left, both, NT, preferred_element_type=jnp.float32)
        out = out[: 2 * n] + out[2 * n :]
        momentum_new[:, at:end] = buffer_ref[:, at:end] - out[:n]
        weight_new[:, at:end] = weight_ref[:, at:end] - out[n:]
        send(momentum_new.at[:, at:end], momentum_out.at[:, at:end])
        send(weight_new.at[:, at:end], weight_out.at[:, at:end])
    for copy in copies:
        copy.wait()


def update(decay, gain, right, left, buffer, weight):
    shapes = (weight.shape, weight.shape, (weight.shape[1], RANK))
    return pl.pallas_call(
        functools.partial(update_kernel, decay, gain),
        out_shape=tuple(jax.ShapeDtypeStruct(shape, jnp.float32) for shape in shapes),
        in_specs=[VM] * 4,
        out_specs=(ANY,) * 3,
        scratch_shapes=[pltpu.VMEM(shape, jnp.float32) for shape in shapes]
        + [pltpu.SemaphoreType.DMA((12,))],
        compiler_params=params(),
        name="update",
    )(right, left, buffer, weight)


def groups(same, order):
    found = {}
    for device in range(X * Y * Z * 2):
        chip, core = divmod(device, 2)
        x, y, z = shifted(chip, core)
        found.setdefault((core, same(x, y, z)), []).append((order(x, y, z), device))
    return [[device for _, device in sorted(members)] for members in found.values()]


def shifted(chip, core):
    return (chip // (Y * Z) + core) % X, (chip // Z % Y + core) % Y, (chip % Z + core) % Z


def cube(x, y, z):
    return x % 2, y % 2, z % 2


def far(x, y, z):
    return y // 2, z // 2


CUBE = groups(lambda x, y, z: (x // 2, y // 2, z // 2), cube)
NEAR = groups(far, lambda x, y, z: (x // 2,) + cube(x, y, z))
FAR = groups(lambda x, y, z: cube(x, y, z) + (x // 2,), far)


def exchange(blocks, members):
    return lax.all_to_all(blocks, ALL, 0, 0, axis_index_groups=members, tiled=True)


def gather(block, members):
    return exchange(jnp.broadcast_to(block[None], (len(members[0]),) + block.shape), members)


def per_device(weight, momentum, grad, right_factor):
    rows, cols = momentum.shape
    n_near, n_far = len(NEAR[0]), len(FAR[0])
    chunk = cols // n_near
    wide = -(-chunk // RANK) * RANK
    piece = chunk // n_far

    buffer = momentum + grad.astype(jnp.float32)
    parts, left_part = head(buffer, right_factor, n_near, wide)
    left_raw = lax.psum(left_part, "tensor")
    beside = jnp.broadcast_to(left_raw[None], (n_near, rows, RANK))
    held = exchange(jnp.concatenate([parts, beside], axis=2), NEAR)

    sent = part_of(held.reshape(n_near * rows, wide + RANK), n_far, piece)
    summed = jnp.sum(exchange(sent, FAR), axis=0)

    by_far = gather(summed, FAR)
    own = by_far[:, :piece].reshape(chunk, RANK)
    count = X * Y * Z
    other = lax.ppermute(own, "dp", [(i, (i + count // 2) % count) for i in range(count)])
    inverse = factor(by_far[:, piece:].reshape(-1, RANK))
    x = (lax.axis_index("dp") // (Y * Z) + lax.axis_index("tensor")) % X
    right, squares, left = right_of((x // 2).reshape(1), own, other, inverse, left_raw)
    squares = lax.psum(squares, "tensor")
    by_cube = gather(jnp.concatenate([right, squares], axis=0), CUBE)
    gain = 0.5 * math.sqrt(count * rows * 2 * cols / RANK)
    return update(1.0 - 0.95, gain, by_cube, left, buffer, weight)


def solution(mesh):
    in_specs = (P("dp", "tensor"), P("dp", "tensor"), P("dp", "tensor"), P("tensor", None))
    out_specs = (P("dp", "tensor"), P("dp", "tensor"), P("tensor", None))
    return jax.shard_map(
        per_device, mesh=mesh, in_specs=in_specs, out_specs=out_specs, check_vma=False
    )
```
